32 devices in a mesh: base: 16 (over z, y, x), facet: 2 (over core).
Axes of the slice: x: 2, y: 2, z: 4, core: 2. Of those that a mesh axis runs over, the one named last changes fastest.
Arguments:
- observed: float32 [2, 4, 64, 4096], P(None, None, None, 'base'), may hold values from -6 to 6
- station_pairs: int32 [2, 4096], P(None, 'base'), may hold values from 0 to 511, as said below
- station_uvw: float32 [4, 3, 512], replicated, may hold values from -40 to 40
- directions: float32 [2, 2, 256], P('facet'), may hold values from -0.3 to 0.3
- fluxes: float32 [2, 256], P('facet'), may hold values from 0.02 to 0.2
- counts: int32 [2], P('facet'), may hold values from 32 to 256, as said below
- jones_gains: float32 [2, 4, 2, 512], P(None, None, 'facet'), may hold values from -2 to 3
Outputs:
- residual: float32 [2, 4, 64, 4096], P(None, None, None, ('base', 'facet'))
- scaled_grad: float32 [2, 4, 2, 512], P(None, None, 'facet')
The draws below stay inside these ranges and needn't reach their ends.
Inputs may be any that keep to these rules, and one draw needn't show every extreme that they name: `station_pairs`: the two stations of a baseline differ. `counts`: some facet holds exactly 256 live components and some other facet fewer.
All inputs are finite; a program needn't handle non-finite values.
Results may differ from the reference program's by a relative error of at most 0.0003.
Values sent between devices are 32-bit elements; how exact they have to be, the bound alone decides.
A program may use at most 64 MiB of HBM per device.

```python
import math
import jax
import jax.numpy as jnp
from jax import lax

STATION_COUNT = 512
INTEGRATION_COUNT = 4
CHANNEL_COUNT = 16
CAP = 256
BASELINE_COUNT = 4096
FACETS = 2


def draw_station_pairs(key, part):
    key = jax.random.fold_in(key, 1)
    first_key, second_key = jax.random.split(key)
    first_station = jax.random.randint(first_key, (BASELINE_COUNT,), 0, STATION_COUNT)
    index_shift = jax.random.randint(second_key, (BASELINE_COUNT,), 1, STATION_COUNT)
    second = (first_station + index_shift) % STATION_COUNT
    return jnp.stack([jnp.minimum(first_station, second), jnp.maximum(first_station, second)]).astype(jnp.int32)


def draw_counts(key, part):
    key = jax.random.fold_in(key, 2)
    first_key, second_key, third_key = jax.random.split(key, 3)
    values = jax.random.randint(first_key, (FACETS,), CAP // 8, CAP + 1)
    fullest = jax.random.randint(second_key, (), 0, FACETS)
    lesser = jax.random.randint(third_key, (), CAP // 8, CAP)
    places = jnp.arange(FACETS)
    values = jnp.where(places == (fullest + 1) % FACETS, lesser, values)
    return jnp.where(places == fullest, CAP, values).astype(jnp.int32)


def draw_jones_gains(key, part):
    key = jax.random.fold_in(key, 3)
    noise = jnp.clip(jax.random.normal(key, (2, 4, FACETS, STATION_COUNT), jnp.float32), -4.0, 4.0)
    noise = noise * 0.3
    identity = jnp.array([1.0, 0.0, 0.0, 1.0], jnp.float32)
    index_shift = jnp.stack([identity, jnp.zeros((4,), jnp.float32)])
    return noise + index_shift[:, :, None, None]


def steps_of(rng, dims, pieces, low, largest):
    level = 1.0
    for position, blocks in pieces:
        draws = jax.random.uniform(jax.random.fold_in(jax.random.fold_in(rng, 6), position), (blocks,), jnp.float32, low / len(pieces), largest / len(pieces))
        level = level * jnp.repeat(jnp.exp(draws), dims[position] // blocks).reshape((-1,) + (1,) * (len(dims) - 1 - position))
    return level


def normal_values(stream_key, extent, scale, most, pieces=(), held_as=jnp.bfloat16):
    drawn = jax.random.normal(stream_key, extent, jnp.float32) * scale
    if len(pieces) > 0:
        drawn = steps_of(stream_key, extent, pieces, -0.22, 0.18) * drawn
    return jnp.clip(drawn, min=-most, max=most).astype(held_as)


def setup_inputs(seed: int = 0) -> dict:
    keys = jax.random.split(jax.random.key(seed), 8)
    observed = normal_values(keys[0], (2, 4, INTEGRATION_COUNT * CHANNEL_COUNT, BASELINE_COUNT), 1.0, 6.0, ((3, 16),), jnp.float32)
    station_pairs = draw_station_pairs(jax.random.fold_in(keys[7], 71), 0)
    station_uvw = normal_values(keys[2], (INTEGRATION_COUNT, 3, STATION_COUNT), 10.0, 40.0, (), jnp.float32)
    directions = jnp.clip(jax.random.uniform(keys[3], (FACETS, 2, CAP), jnp.float32, -0.3, 0.3) * steps_of(keys[3], (FACETS, 2, CAP), ((0, 2),), -0.4, 0.0), -0.3, 0.3)
    fluxes = jnp.clip(jnp.exp(math.log(0.2) - 2.3025851 * jax.random.uniform(keys[4], (FACETS, CAP), jnp.float32) ** steps_of(keys[4], (FACETS, CAP), ((0, 2),), -0.2, 0.2)), 0.02, 0.2)
    counts = draw_counts(jax.random.fold_in(keys[7], 71), 0)
    jones_gains = draw_jones_gains(jax.random.fold_in(keys[7], 71), 0)
    return dict(observed=observed, station_pairs=station_pairs, station_uvw=station_uvw, directions=directions, fluxes=fluxes, counts=counts, jones_gains=jones_gains)


def mat_mul(left_mat, right_mat):
    left_re, left_im = left_mat
    right_re, right_im = right_mat
    real_part = left_re[:, 0:1] * right_re[0:1, :] + left_re[:, 1:2] * right_re[1:2, :] - left_im[:, 0:1] * right_im[0:1, :] - left_im[:, 1:2] * right_im[1:2, :]
    imag_part = left_re[:, 0:1] * right_im[0:1, :] + left_re[:, 1:2] * right_im[1:2, :] + left_im[:, 0:1] * right_re[0:1, :] + left_im[:, 1:2] * right_re[1:2, :]
    return (real_part, imag_part)

def adjoint(matrix):
    return (jnp.swapaxes(matrix[0], 0, 1), -jnp.swapaxes(matrix[1], 0, 1))

def base_phase(uvw, dirs):
    dir_l = dirs[0]
    dir_m = dirs[1]
    depth_term = jnp.sqrt(1.0 - dir_l * dir_l - dir_m * dir_m) - 1.0
    return 2.0 * math.pi * (uvw[:, 0, None, :] * dir_l[None, :, None] + uvw[:, 1, None, :] * dir_m[None, :, None] + uvw[:, 2, None, :] * depth_term[None, :, None])

def predict(uvw, dirs, weights):
    phase = base_phase(uvw, dirs)
    freq_ratio = 1.0 + jnp.arange(CHANNEL_COUNT).astype(jnp.float32) / (2.0 * CHANNEL_COUNT)

    def one_time(phase_slab):
        angles = freq_ratio[:, None, None] * phase_slab[None]
        real_part = jnp.einsum('c,fcb->fb', weights, jnp.cos(angles), precision=lax.Precision.HIGHEST)
        imag_part = -jnp.einsum('c,fcb->fb', weights, jnp.sin(angles), precision=lax.Precision.HIGHEST)
        return (real_part, imag_part)
    real_part, imag_part = lax.map(one_time, phase)
    return (real_part.reshape(INTEGRATION_COUNT * CHANNEL_COUNT, -1), imag_part.reshape(INTEGRATION_COUNT * CHANNEL_COUNT, -1))

def flatten(matrix):
    return jnp.concatenate([matrix[0].reshape(4, -1), matrix[1].reshape(4, -1)], axis=0)

def reference(observed, station_pairs, station_uvw, directions, fluxes, counts, jones_gains):
    first_station = station_pairs[0]
    second = station_pairs[1]
    slots = jnp.arange(CAP).astype(jnp.int32)
    live = fluxes * (slots[None, :] < counts[:, None]).astype(jnp.float32)
    uvw = station_uvw[:, :, first_station] - station_uvw[:, :, second]
    models = []
    gains = []
    real_total = jnp.zeros((2, 2, INTEGRATION_COUNT * CHANNEL_COUNT, BASELINE_COUNT), jnp.float32)
    imaginary_total = jnp.zeros((2, 2, INTEGRATION_COUNT * CHANNEL_COUNT, BASELINE_COUNT), jnp.float32)
    for index in range(FACETS):
        model_re, model_im = predict(uvw, directions[index], live[index])
        jre = jones_gains[0, :, index, :].reshape(2, 2, STATION_COUNT)
        jim = jones_gains[1, :, index, :].reshape(2, 2, STATION_COUNT)
        jones_p = (jre[:, :, first_station], jim[:, :, first_station])
        jones_q = (jre[:, :, second], jim[:, :, second])
        prod_re, prod_im = mat_mul(jones_p, adjoint(jones_q))
        real_total = real_total + model_re * prod_re[:, :, None, :] - model_im * prod_im[:, :, None, :]
        imaginary_total = imaginary_total + model_re * prod_im[:, :, None, :] + model_im * prod_re[:, :, None, :]
        models.append((model_re, model_im))
        gains.append((jones_p, jones_q))
    residual_real = observed[0].reshape(2, 2, INTEGRATION_COUNT * CHANNEL_COUNT, BASELINE_COUNT) - real_total
    residual_imaginary = observed[1].reshape(2, 2, INTEGRATION_COUNT * CHANNEL_COUNT, BASELINE_COUNT) - imaginary_total
    residual = jnp.stack([residual_real.reshape(4, INTEGRATION_COUNT * CHANNEL_COUNT, BASELINE_COUNT), residual_imaginary.reshape(4, INTEGRATION_COUNT * CHANNEL_COUNT, BASELINE_COUNT)])
    results = []
    for index in range(FACETS):
        model_re, model_im = models[index]
        jones_p, jones_q = gains[index]
        acc_re = lax.optimization_barrier(jnp.sum(model_re * residual_real + model_im * residual_imaginary, axis=2))
        acc_im = lax.optimization_barrier(jnp.sum(model_re * residual_imaginary - model_im * residual_real, axis=2))
        grad_p = -flatten(mat_mul((acc_re, acc_im), jones_q))
        grad_q = -flatten(mat_mul(adjoint((acc_re, acc_im)), jones_p))
        power = lax.optimization_barrier(jnp.sum(model_re * model_re + model_im * model_im, axis=0))
        norm_p = lax.optimization_barrier(jnp.sum(jones_p[0] * jones_p[0] + jones_p[1] * jones_p[1], axis=(0, 1)))
        norm_q = lax.optimization_barrier(jnp.sum(jones_q[0] * jones_q[0] + jones_q[1] * jones_q[1], axis=(0, 1)))
        grads = jax.ops.segment_sum(grad_p.T, first_station, num_segments=STATION_COUNT).T + jax.ops.segment_sum(grad_q.T, second, num_segments=STATION_COUNT).T
        weight = jax.ops.segment_sum(power * norm_q, first_station, num_segments=STATION_COUNT) + jax.ops.segment_sum(power * norm_p, second, num_segments=STATION_COUNT)
        scaled = grads / (jnp.sqrt(weight)[None, :] + 1.0)
        results.append(scaled.reshape(2, 4, STATION_COUNT))
    return (residual, jnp.stack(results, axis=2))
```

```python
import functools
import math

import jax
import jax.numpy as jnp
from jax import lax
from jax.experimental import pallas as pl
from jax.experimental.pallas import tpu as pltpu
from jax.sharding import PartitionSpec as P

MESH = pl.DeviceIdType.MESH
LANES = 128
TIMES = 4
CHANNELS = 16
ROWS = 9
STEP = 16
VMEM = pltpu.MemorySpace.VMEM
SMEM = pltpu.MemorySpace.SMEM

SIN = (4.442882919124344, -7.308245686509057, 3.6063542184328345, -0.846111650373896, 0.10982451642611356)
COS = (1.4142134962552284, -6.978850948563788, 5.73946037690675, -1.8835579059841707, 0.3106880275217573)


def poly(x, coefficients):
    value = coefficients[-1]
    for c in coefficients[-2::-1]:
        value = value * x + c
    return value


def cos_sin_turns(turns):
    magic = 12582912.0
    r = turns - ((turns + magic) - magic)
    x = r * r
    half_sin = r * poly(x, SIN)
    half_cos = poly(x, COS)
    return 1.0 - half_sin * half_sin, half_sin * half_cos


def split3(a):
    high = a.astype(jnp.bfloat16)
    rest = a - high.astype(jnp.float32)
    mid = rest.astype(jnp.bfloat16)
    low = (rest - mid.astype(jnp.float32)).astype(jnp.bfloat16)
    return high, mid, low


def exact_dot(a, hot, dims):
    out = None
    for part in split3(a):
        term = lax.dot_general(part, hot, (dims, ((), ())), preferred_element_type=jnp.float32)
        out = term if out is None else out + term
    return out


def product(a, b):
    out = []
    for i in range(2):
        for j in range(2):
            re = im = None
            for k in range(2):
                (x, y), (u, v) = a[2 * i + k], b[2 * k + j]
                r, s = x * u - y * v, x * v + y * u
                re, im = (r, s) if re is None else (re + r, im + s)
            out.append((re, im))
    return out


def adjoint(a):
    return [(a[i][0], -a[i][1]) for i in (0, 2, 1, 3)]


def share_kernel(facets, directions_ref, fluxes_ref, counts_ref, gains_ref, out_ref, send_sem, recv_sem):
    me = lax.axis_index("facet")
    barrier = pltpu.get_barrier_semaphore()
    for d in range(1, facets):
        pl.semaphore_signal(barrier, inc=1, device_id={"facet": lax.rem(me + d, facets)}, device_id_type=MESH)
    cap = fluxes_ref.shape[1]
    count = counts_ref[0]
    out_ref[me] = jnp.zeros(out_ref.shape[1:], jnp.float32)
    for i in range(2):
        for j in range(4):
            out_ref[me, 4 * i + j : 4 * i + j + 1, :] = gains_ref[i, j]
    l = directions_ref[0, 0:1, :]
    m = directions_ref[0, 1:2, :]
    slots = lax.broadcasted_iota(jnp.int32, (1, cap), 1)
    out_ref[me, 8:9, 0:cap] = l
    out_ref[me, 9:10, 0:cap] = m
    out_ref[me, 10:11, 0:cap] = jnp.sqrt(1.0 - l * l - m * m) - 1.0
    out_ref[me, 11:12, 0:cap] = jnp.where(slots < count, fluxes_ref[...], 0.0)
    out_ref[me, 12:13, 0:cap] = jnp.full((1, cap), count, jnp.int32).astype(jnp.float32)
    pl.semaphore_wait(barrier, facets - 1)
    copies = []
    for d in range(1, facets):
        copy = pltpu.make_async_remote_copy(
            src_ref=out_ref.at[me],
            dst_ref=out_ref.at[me],
            send_sem=send_sem.at[d - 1],
            recv_sem=recv_sem.at[d - 1],
            device_id={"facet": lax.rem(me + d, facets)},
            device_id_type=MESH,
        )
        copy.start()
        copies.append(copy)
    for d, copy in enumerate(copies, 1):
        copy.wait_send()
        other = lax.rem(me + facets - d, facets)
        pltpu.make_async_remote_copy(
            src_ref=out_ref.at[me],
            dst_ref=out_ref.at[other],
            send_sem=send_sem.at[d - 1],
            recv_sem=recv_sem.at[d - 1],
            device_id={"facet": other},
            device_id_type=MESH,
        ).wait_recv()


def model_kernel(facets, sliced, cap, facet_ref, observed_ref, pairs_ref, uvw_ref, params_ref, out_ref, part_ref,
                 table, gathered, hot, base, angle, model, left, copy_sem):
    width = out_ref.shape[3]
    stations = uvw_ref.shape[2]
    groups = stations // LANES
    start = pl.multiple_of(facet_ref[0] * width, LANES)
    source = observed_ref.at[:, :, :, pl.ds(start, width)] if sliced else observed_ref
    copy = pltpu.make_async_copy(source, out_ref, copy_sem)
    copy.start()
    if sliced:
        pairs = pairs_ref[:, pl.ds(start, width)]
    else:
        pairs = pairs_ref[...]
    column = lax.broadcasted_iota(jnp.int32, (stations, width), 0)
    for side in range(2):
        hot[side] = (column == pairs[side : side + 1, :]).astype(jnp.float32).astype(jnp.bfloat16)
    for t in range(TIMES):
        table[8 * t : 8 * t + 3, :] = uvw_ref[t]
        table[8 * t + 3 : 8 * t + 8, :] = jnp.zeros((5, stations), jnp.float32)
    for k in range(facets):
        table[32 + 8 * k : 40 + 8 * k, :] = params_ref[k, 0:8, :]
    for side in range(2):
        gathered[side] = exact_dot(table[...], hot[side], ((1,), (0,)))
    for t in range(TIMES):
        base[:, t * width : (t + 1) * width] = gathered[0, 8 * t : 8 * t + 8, :] - gathered[1, 8 * t : 8 * t + 8, :]
    row = lax.broadcasted_iota(jnp.int32, (8, width), 0)
    base[:, TIMES * width :] = (row == 3).astype(jnp.float32)

    def jones(k, side):
        rows = gathered[side, pl.ds(pl.multiple_of(32 + 8 * k, 8), 8), :]
        return [(rows[e : e + 1, :], rows[4 + e : 5 + e, :]) for e in range(4)]

    def facet_model(k, carry):
        slots = jnp.transpose(params_ref[k, 8:16, 0:cap])
        angle[...] = jnp.dot(slots, base[...], precision=lax.Precision.HIGHEST, preferred_element_type=jnp.float32)
        count = jnp.max(params_ref[k, 12:13, 0:LANES]).astype(jnp.int32)
        steps = (count + STEP - 1) // STEP
        for t in range(TIMES):

            def step(i, acc):
                rows = pl.ds(pl.multiple_of(i * STEP, STEP), STEP)
                turns = angle[rows, t * width : (t + 1) * width]
                live = angle[rows, TIMES * width :]
                cz, sz = cos_sin_turns(turns * (79.0 / 64.0))
                c0, s0 = cos_sin_turns(turns * (1.0 / 64.0))
                cz, sz = cz * live, sz * live
                twice = 4.0 * (c0 * c0) - 2.0
                cs, ss = [c0, (twice - 1.0) * c0], [s0, (twice + 1.0) * s0]
                for j in range(2):
                    cs.append(twice * cs[-1] - cs[-2])
                    ss.append(twice * ss[-1] - ss[-2])
                c4 = cs[3] * c0 - ss[3] * s0
                s4 = ss[3] * c0 + cs[3] * s0
                cc, sn, sc, cn = cz * c4, sz * s4, sz * c4, cz * s4
                centres = ((cc + sn, sc - cn), (cc - sn, sc + cn))
                out = []
                for a, b in centres:
                    for j in range(4):
                        for value in (a * cs[j], b * ss[j], a * ss[j], b * cs[j]):
                            out.append(acc[len(out)] + (value[0:8] + value[8:16]))
                return tuple(out)

            zero = jnp.zeros((8, width), jnp.float32)
            acc = lax.fori_loop(0, steps, step, (zero,) * 32)
            real, imaginary = [None] * CHANNELS, [None] * CHANNELS
            for centre in range(2):
                for j in range(4):
                    p = acc[16 * centre + 4 * j : 16 * centre + 4 * j + 4]
                    up, down = 8 * centre + 4 + j, 8 * centre + 3 - j
                    real[up], real[down] = p[0] - p[1], p[0] + p[1]
                    imaginary[up], imaginary[down] = -(p[2] + p[3]), p[2] - p[3]
            for part, values in enumerate((real, imaginary)):
                sums = [jnp.sum(v, axis=0, keepdims=True) for v in values]
                model[k, part, CHANNELS * t : CHANNELS * (t + 1), :] = jnp.concatenate(sums, axis=0)
        return carry

    lax.fori_loop(0, facets, facet_model, 0)
    copy.wait()

    def subtract(k, carry):
        prod = product(jones(k, 0), adjoint(jones(k, 1)))
        re, im = model[k, 0], model[k, 1]
        for e, (x, y) in enumerate(prod):
            out_ref[0, e] = out_ref[0, e] - (re * x - im * y)
            out_ref[1, e] = out_ref[1, e] - (re * y + im * x)
        return carry

    lax.fori_loop(0, facets, subtract, 0)

    def terms(k, carry):
        re, im = model[k, 0], model[k, 1]
        acc = []
        for e in range(4):
            x, y = out_ref[0, e], out_ref[1, e]
            acc.append((jnp.sum(re * x + im * y, axis=0, keepdims=True), jnp.sum(re * y - im * x, axis=0, keepdims=True)))
        power = jnp.sum(re * re + im * im, axis=0, keepdims=True)
        first, second = jones(k, 0), jones(k, 1)
        for side, (grad, other) in enumerate(((product(acc, second), second), (product(adjoint(acc), first), first))):
            norm = None
            for x, y in other:
                norm = x * x + y * y if norm is None else norm + (x * x + y * y)
            rows = [-grad[e][0] for e in range(4)] + [-grad[e][1] for e in range(4)] + [power * norm]
            left[side, pl.ds(pl.multiple_of(16 * k, 16), 16), :] = jnp.concatenate(
                rows + [jnp.zeros((7, width), jnp.float32)], axis=0)
        return carry

    lax.fori_loop(0, facets, terms, 0)
    sums = None
    for side in range(2):
        term = exact_dot(left[side], hot[side], ((1,), (1,)))
        sums = term if sums is None else sums + term
    for k in range(facets):
        for r in range(ROWS):
            for g in range(groups):
                part_ref[k, r, g : g + 1, :] = sums[16 * k + r : 16 * k + r + 1, g * LANES : (g + 1) * LANES]


def reduce_kernel(blocks, facets, part_ref, out_ref, inbox, totals, send_sem, recv_sem, spread_sem, total_sem):
    b = lax.axis_index("base")
    f = lax.axis_index("facet")
    devices = blocks * facets
    me = b * facets + f
    first = (blocks - ROWS) // 2
    groups = part_ref.shape[2]
    barrier = pltpu.get_barrier_semaphore()

    def greet(d, carry):
        other = lax.rem(me + d, devices)
        pl.semaphore_signal(barrier, inc=1, device_id=(other // facets, lax.rem(other, facets)), device_id_type=MESH)
        return carry

    lax.fori_loop(1, devices, greet, 0)
    pl.semaphore_wait(barrier, devices - 1)

    def outgoing(i):
        r, k = i // facets, lax.rem(i, facets)
        target = (first + r) * facets + k
        slot = lax.rem(me - target + devices, devices) - 1
        return target, r, k, slot

    def send(i, carry):
        target, r, k, slot = outgoing(i)

        @pl.when(target != me)
        def _():
            pltpu.make_async_remote_copy(
                src_ref=part_ref.at[k, r], dst_ref=inbox.at[slot], send_sem=send_sem.at[i], recv_sem=recv_sem.at[slot],
                device_id=(first + r, k), device_id_type=MESH).start()

        return carry

    lax.fori_loop(0, ROWS * facets, send, 0)
    row = b - first

    @pl.when(jnp.logical_and(row >= 0, row < ROWS))
    def _():
        def receive(s, carry):
            pltpu.make_async_copy(inbox.at[s], inbox.at[s], recv_sem.at[s]).wait()
            return carry

        lax.fori_loop(0, devices - 1, receive, 0)
        totals[row] = jnp.sum(inbox[...], axis=0) + part_ref[f, row]

        def spread(d, carry):
            pltpu.make_async_remote_copy(
                src_ref=totals.at[row], dst_ref=totals.at[row], send_sem=spread_sem.at[d - 1], recv_sem=total_sem.at[row],
                device_id=(lax.rem(b + d, blocks), f), device_id_type=MESH).start()
            return carry

        lax.fori_loop(1, blocks, spread, 0)

    def arrive(r, carry):
        @pl.when(r != row)
        def _():
            pltpu.make_async_copy(totals.at[r], totals.at[r], total_sem.at[r]).wait()

        return carry

    lax.fori_loop(0, ROWS, arrive, 0)
    scale = 1.0 / (jnp.sqrt(totals[ROWS - 1]) + 1.0)
    for i in range(2):
        for j in range(4):
            value = totals[4 * i + j] * scale
            for g in range(groups):
                out_ref[i, j, 0:1, g * LANES : (g + 1) * LANES] = value[g : g + 1, :]

    def sent(i, carry):
        target, r, k, slot = outgoing(i)

        @pl.when(target != me)
        def _():
            pltpu.make_async_copy(part_ref.at[k, r], part_ref.at[k, r], send_sem.at[i]).wait()

        return carry

    lax.fori_loop(0, ROWS * facets, sent, 0)

    @pl.when(jnp.logical_and(row >= 0, row < ROWS))
    def _():
        def spread_done(d, carry):
            pltpu.make_async_copy(totals.at[row], totals.at[row], spread_sem.at[d - 1]).wait()
            return carry

        lax.fori_loop(1, blocks, spread_done, 0)


def body(blocks, facets, observed, station_pairs, station_uvw, directions, fluxes, counts, jones_gains):
    f32 = jnp.float32
    stations = jones_gains.shape[3]
    cap = fluxes.shape[1]
    samples = observed.shape[2]
    share = observed.shape[3] // facets
    vmem = pl.BlockSpec(memory_space=VMEM)
    smem = pl.BlockSpec(memory_space=SMEM)
    params = pl.pallas_call(
        functools.partial(share_kernel, facets),
        out_shape=jax.ShapeDtypeStruct((facets, 16, stations), f32),
        in_specs=[vmem, vmem, smem, vmem],
        out_specs=vmem,
        scratch_shapes=[pltpu.SemaphoreType.DMA((facets - 1,)), pltpu.SemaphoreType.DMA((facets - 1,))],
        compiler_params=pltpu.CompilerParams(collective_id=0, has_side_effects=True),
        name="share_parameters",
    )(directions, fluxes, counts, jones_gains)
    facet = lax.axis_index("facet").astype(jnp.int32)
    width = -(-share // LANES) * LANES
    sliced = width == share
    if not sliced:
        pad = width - share
        observed = lax.dynamic_slice_in_dim(observed, facet * share, share, 3)
        station_pairs = lax.dynamic_slice_in_dim(station_pairs, facet * share, share, 1)
        observed = jnp.pad(observed, ((0, 0),) * 3 + ((0, pad),))
        station_pairs = jnp.pad(station_pairs, ((0, 0), (0, pad)), constant_values=-1)
    residual, part = pl.pallas_call(
        functools.partial(model_kernel, facets, sliced, cap),
        out_shape=(
            jax.ShapeDtypeStruct((2, 4, samples, width), f32),
            jax.ShapeDtypeStruct((facets, ROWS, stations // LANES, LANES), f32),
        ),
        in_specs=[smem, pl.BlockSpec(memory_space=pl.ANY), vmem, vmem, vmem],
        out_specs=(vmem, vmem),
        scratch_shapes=[
            pltpu.VMEM((32 + 8 * facets, stations), f32),
            pltpu.VMEM((2, 32 + 8 * facets, width), f32),
            pltpu.VMEM((2, stations, width), jnp.bfloat16),
            pltpu.VMEM((8, (TIMES + 1) * width), f32),
            pltpu.VMEM((cap, (TIMES + 1) * width), f32),
            pltpu.VMEM((facets, 2, samples, width), f32),
            pltpu.VMEM((2, 16 * facets, width), f32),
            pltpu.SemaphoreType.DMA,
        ],
        compiler_params=pltpu.CompilerParams(vmem_limit_bytes=32 * 2**20),
        name="model_and_residual",
    )(facet.reshape(1), observed, station_pairs, station_uvw, params)
    if not sliced:
        residual = residual[..., :share]
    scaled = pl.pallas_call(
        functools.partial(reduce_kernel, blocks, facets),
        out_shape=jax.ShapeDtypeStruct((2, 4, 1, stations), f32),
        in_specs=[vmem],
        out_specs=vmem,
        scratch_shapes=[
            pltpu.VMEM((blocks * facets - 1, stations // LANES, LANES), f32),
            pltpu.VMEM((ROWS, stations // LANES, LANES), f32),
            pltpu.SemaphoreType.DMA((ROWS * facets,)),
            pltpu.SemaphoreType.DMA((blocks * facets - 1,)),
            pltpu.SemaphoreType.DMA((blocks - 1,)),
            pltpu.SemaphoreType.DMA((ROWS,)),
        ],
        compiler_params=pltpu.CompilerParams(collective_id=1, has_side_effects=True),
        name="sum_stations",
    )(part)
    return residual, scaled


def solution(mesh):
    placed = (
        P(None, None, None, "base"),
        P(None, "base"),
        P(),
        P("facet", None, None),
        P("facet", None),
        P("facet"),
        P(None, None, "facet", None),
    )
    return jax.shard_map(
        functools.partial(body, mesh.shape["base"], mesh.shape["facet"]),
        mesh=mesh,
        in_specs=placed,
        out_specs=(P(None, None, None, ("base", "facet")), P(None, None, "facet", None)),
        check_vma=False,
    )
```

```python
import functools
import math

import jax
import jax.numpy as jnp
from jax import lax
from jax.experimental import pallas as pl
from jax.experimental.pallas import tpu as pltpu
from jax.sharding import PartitionSpec as P

MESH = pl.DeviceIdType.MESH
LANES = 128
TIMES = 4
CHANNELS = 16
ROWS = 9
STEP = 16
VMEM = pltpu.MemorySpace.VMEM
SMEM = pltpu.MemorySpace.SMEM

SIN = (4.442882919124344, -7.308245686509057, 3.6063542184328345, -0.846111650373896, 0.10982451642611356)
COS = (1.4142134962552284, -6.978850948563788, 5.73946037690675, -1.8835579059841707, 0.3106880275217573)


def poly(x, coefficients):
    value = coefficients[-1]
    for c in coefficients[-2::-1]:
        value = value * x + c
    return value


def cos_sin_turns(turns):
    magic = 12582912.0
    r = turns - ((turns + magic) - magic)
    x = r * r
    half_sin = r * poly(x, SIN)
    half_cos = poly(x, COS)
    return 1.0 - half_sin * half_sin, half_sin * half_cos


def split3(a):
    high = a.astype(jnp.bfloat16)
    rest = a - high.astype(jnp.float32)
    mid = rest.astype(jnp.bfloat16)
    low = (rest - mid.astype(jnp.float32)).astype(jnp.bfloat16)
    return high, mid, low


def exact_dot(a, hot, dims):
    out = None
    for part in split3(a):
        term = lax.dot_general(part, hot, (dims, ((), ())), preferred_element_type=jnp.float32)
        out = term if out is None else out + term
    return out


def product(a, b):
    out = []
    for i in range(2):
        for j in range(2):
            re = im = None
            for k in range(2):
                (x, y), (u, v) = a[2 * i + k], b[2 * k + j]
                r, s = x * u - y * v, x * v + y * u
                re, im = (r, s) if re is None else (re + r, im + s)
            out.append((re, im))
    return out


def adjoint(a):
    return [(a[i][0], -a[i][1]) for i in (0, 2, 1, 3)]


def share_kernel(facets, directions_ref, fluxes_ref, counts_ref, gains_ref, out_ref, send_sem, recv_sem):
    me = lax.axis_index("facet")
    barrier = pltpu.get_barrier_semaphore()
    for d in range(1, facets):
        pl.semaphore_signal(barrier, inc=1, device_id={"facet": lax.rem(me + d, facets)}, device_id_type=MESH)
    cap = fluxes_ref.shape[1]
    count = counts_ref[0]
    out_ref[me] = jnp.zeros(out_ref.shape[1:], jnp.float32)
    for i in range(2):
        for j in range(4):
            out_ref[me, 4 * i + j : 4 * i + j + 1, :] = gains_ref[i, j]
    l = directions_ref[0, 0:1, :]
    m = directions_ref[0, 1:2, :]
    slots = lax.broadcasted_iota(jnp.int32, (1, cap), 1)
    out_ref[me, 8:9, 0:cap] = l
    out_ref[me, 9:10, 0:cap] = m
    out_ref[me, 10:11, 0:cap] = jnp.sqrt(1.0 - l * l - m * m) - 1.0
    out_ref[me, 11:12, 0:cap] = jnp.where(slots < count, fluxes_ref[...], 0.0)
    out_ref[me, 12:13, 0:cap] = jnp.full((1, cap), count, jnp.int32).astype(jnp.float32)
    pl.semaphore_wait(barrier, facets - 1)
    copies = []
    for d in range(1, facets):
        copy = pltpu.make_async_remote_copy(
            src_ref=out_ref.at[me],
            dst_ref=out_ref.at[me],
            send_sem=send_sem.at[d - 1],
            recv_sem=recv_sem.at[d - 1],
            device_id={"facet": lax.rem(me + d, facets)},
            device_id_type=MESH,
        )
        copy.start()
        copies.append(copy)
    for d, copy in enumerate(copies, 1):
        copy.wait_send()
        other = lax.rem(me + facets - d, facets)
        pltpu.make_async_remote_copy(
            src_ref=out_ref.at[me],
            dst_ref=out_ref.at[other],
            send_sem=send_sem.at[d - 1],
            recv_sem=recv_sem.at[d - 1],
            device_id={"facet": other},
            device_id_type=MESH,
        ).wait_recv()


def model_kernel(facets, sliced, cap, facet_ref, observed_ref, pairs_ref, uvw_ref, params_ref, out_ref, part_ref,
                 table, gathered, hot, base, angle, model, left, copy_sem):
    width = out_ref.shape[3]
    stations = uvw_ref.shape[2]
    groups = stations // LANES
    start = pl.multiple_of(facet_ref[0] * width, LANES)
    source = observed_ref.at[:, :, :, pl.ds(start, width)] if sliced else observed_ref
    copy = pltpu.make_async_copy(source, out_ref, copy_sem)
    copy.start()
    if sliced:
        pairs = pairs_ref[:, pl.ds(start, width)]
    else:
        pairs = pairs_ref[...]
    column = lax.broadcasted_iota(jnp.int32, (stations, width), 0)
    for side in range(2):
        hot[side] = (column == pairs[side : side + 1, :]).astype(jnp.float32).astype(jnp.bfloat16)
    for t in range(TIMES):
        for axis in range(3):
            table[8 * t + axis : 8 * t + axis + 1, :] = uvw_ref[axis, t : t + 1, :]
        table[8 * t + 3 : 8 * t + 8, :] = jnp.zeros((5, stations), jnp.float32)
    for k in range(facets):
        table[32 + 8 * k : 40 + 8 * k, :] = params_ref[k, 0:8, :]
    for side in range(2):
        gathered[side] = exact_dot(table[...], hot[side], ((1,), (0,)))
    for t in range(TIMES):
        base[:, t * width : (t + 1) * width] = gathered[0, 8 * t : 8 * t + 8, :] - gathered[1, 8 * t : 8 * t + 8, :]
    row = lax.broadcasted_iota(jnp.int32, (8, width), 0)
    base[:, TIMES * width :] = (row == 3).astype(jnp.float32)

    def jones(k, side):
        rows = gathered[side, pl.ds(pl.multiple_of(32 + 8 * k, 8), 8), :]
        return [(rows[e : e + 1, :], rows[4 + e : 5 + e, :]) for e in range(4)]

    def facet_model(k, carry):
        slots = jnp.transpose(params_ref[k, 8:16, 0:cap])
        angle[...] = jnp.dot(slots, base[...], precision=lax.Precision.HIGHEST, preferred_element_type=jnp.float32)
        count = jnp.max(params_ref[k, 12:13, 0:LANES]).astype(jnp.int32)
        steps = (count + STEP - 1) // STEP
        for t in range(TIMES):

            def step(i, acc):
                rows = pl.ds(pl.multiple_of(i * STEP, STEP), STEP)
                turns = angle[rows, t * width : (t + 1) * width]
                live = angle[rows, TIMES * width :]
                cz, sz = cos_sin_turns(turns * (79.0 / 64.0))
                c0, s0 = cos_sin_turns(turns * (1.0 / 64.0))
                cz, sz = cz * live, sz * live
                twice = 4.0 * (c0 * c0) - 2.0
                cs, ss = [c0, (twice - 1.0) * c0], [s0, (twice + 1.0) * s0]
                for j in range(2):
                    cs.append(twice * cs[-1] - cs[-2])
                    ss.append(twice * ss[-1] - ss[-2])
                c4 = cs[3] * c0 - ss[3] * s0
                s4 = ss[3] * c0 + cs[3] * s0
                cc, sn, sc, cn = cz * c4, sz * s4, sz * c4, cz * s4
                centres = ((cc + sn, sc - cn), (cc - sn, sc + cn))
                out = []
                for a, b in centres:
                    for j in range(4):
                        for value in (a * cs[j], b * ss[j], a * ss[j], b * cs[j]):
                            out.append(acc[len(out)] + (value[0:8] + value[8:16]))
                return tuple(out)

            zero = jnp.zeros((8, width), jnp.float32)
            acc = lax.fori_loop(0, steps, step, (zero,) * 32)
            real, imaginary = [None] * CHANNELS, [None] * CHANNELS
            for centre in range(2):
                for j in range(4):
                    p = acc[16 * centre + 4 * j : 16 * centre + 4 * j + 4]
                    up, down = 8 * centre + 4 + j, 8 * centre + 3 - j
                    real[up], real[down] = p[0] - p[1], p[0] + p[1]
                    imaginary[up], imaginary[down] = -(p[2] + p[3]), p[2] - p[3]
            for part, values in enumerate((real, imaginary)):
                sums = [jnp.sum(v, axis=0, keepdims=True) for v in values]
                model[k, part, CHANNELS * t : CHANNELS * (t + 1), :] = jnp.concatenate(sums, axis=0)
        return carry

    lax.fori_loop(0, facets, facet_model, 0)
    copy.wait()

    def subtract(k, carry):
        prod = product(jones(k, 0), adjoint(jones(k, 1)))
        re, im = model[k, 0], model[k, 1]
        for e, (x, y) in enumerate(prod):
            out_ref[0, e] = out_ref[0, e] - (re * x - im * y)
            out_ref[1, e] = out_ref[1, e] - (re * y + im * x)
        return carry

    lax.fori_loop(0, facets, subtract, 0)

    def terms(k, carry):
        re, im = model[k, 0], model[k, 1]
        acc = []
        for e in range(4):
            x, y = out_ref[0, e], out_ref[1, e]
            acc.append((jnp.sum(re * x + im * y, axis=0, keepdims=True), jnp.sum(re * y - im * x, axis=0, keepdims=True)))
        power = jnp.sum(re * re + im * im, axis=0, keepdims=True)
        first, second = jones(k, 0), jones(k, 1)
        for side, (grad, other) in enumerate(((product(acc, second), second), (product(adjoint(acc), first), first))):
            norm = None
            for x, y in other:
                norm = x * x + y * y if norm is None else norm + (x * x + y * y)
            rows = [-grad[e][0] for e in range(4)] + [-grad[e][1] for e in range(4)] + [power * norm]
            left[side, pl.ds(pl.multiple_of(16 * k, 16), 16), :] = jnp.concatenate(
                rows + [jnp.zeros((7, width), jnp.float32)], axis=0)
        return carry

    lax.fori_loop(0, facets, terms, 0)
    sums = None
    for side in range(2):
        term = exact_dot(left[side], hot[side], ((1,), (1,)))
        sums = term if sums is None else sums + term
    for k in range(facets):
        for r in range(ROWS):
            for g in range(groups):
                part_ref[k, r, g : g + 1, :] = sums[16 * k + r : 16 * k + r + 1, g * LANES : (g + 1) * LANES]


def radices(blocks):
    out = []
    while blocks > 1:
        out.append(4 if blocks % 4 == 0 else blocks)
        blocks //= out[-1]
    return out


def reduce_kernel(blocks, facets, part_ref, out_ref, mine, other_parts, *refs):
    stages = radices(blocks)
    inboxes = refs[: len(stages)]
    send_sem, recv_sem = refs[len(stages) :]
    b = lax.axis_index("base")
    f = lax.axis_index("facet")
    peers = [[(b, lax.rem(f + d, facets)) for d in range(1, facets)]]
    stride = 1
    for radix in stages:
        digit = lax.rem(b // stride, radix)
        low = b - digit * stride
        peers.append([(low + lax.rem(digit + d, radix) * stride, f) for d in range(1, radix)])
        stride *= radix
    barrier = pltpu.get_barrier_semaphore()
    total = 0
    for group in peers:
        for peer in group:
            pl.semaphore_signal(barrier, inc=1, device_id=peer, device_id_type=MESH)
            total += 1
    pl.semaphore_wait(barrier, total)
    copies = []

    def exchange(group, source_of, inbox):
        base = len(copies)
        for d, peer in enumerate(group):
            copy = pltpu.make_async_remote_copy(
                src_ref=source_of(peer), dst_ref=inbox.at[d], send_sem=send_sem.at[base + d],
                recv_sem=recv_sem.at[base + d], device_id=peer, device_id_type=MESH)
            copy.start()
            copies.append(copy)
        for copy in copies[base:]:
            copy.wait_recv()

    exchange(peers[0], lambda peer: part_ref.at[peer[1]], other_parts)
    value = part_ref[f]
    for d in range(len(peers[0])):
        value = value + other_parts[d]
    for s, inbox in enumerate(inboxes):
        mine[s] = value
        exchange(peers[s + 1], lambda peer: mine.at[s], inbox)
        for d in range(len(peers[s + 1])):
            value = value + inbox[d]
    out_ref[...] = value
    for copy in copies:
        copy.wait_send()


def body(blocks, facets, observed, station_pairs, station_uvw, directions, fluxes, counts, jones_gains):
    f32 = jnp.float32
    stations = jones_gains.shape[3]
    cap = fluxes.shape[1]
    samples = observed.shape[2]
    share = observed.shape[3] // facets
    vmem = pl.BlockSpec(memory_space=VMEM)
    smem = pl.BlockSpec(memory_space=SMEM)
    params = pl.pallas_call(
        functools.partial(share_kernel, facets),
        out_shape=jax.ShapeDtypeStruct((facets, 16, stations), f32),
        in_specs=[vmem, vmem, smem, vmem],
        out_specs=vmem,
        scratch_shapes=[pltpu.SemaphoreType.DMA((facets - 1,)), pltpu.SemaphoreType.DMA((facets - 1,))],
        compiler_params=pltpu.CompilerParams(collective_id=0, has_side_effects=True),
        name="share_parameters",
    )(directions, fluxes, counts, jones_gains)
    facet = lax.axis_index("facet").astype(jnp.int32)
    width = -(-share // LANES) * LANES
    sliced = width == share
    if not sliced:
        pad = width - share
        observed = lax.dynamic_slice_in_dim(observed, facet * share, share, 3)
        station_pairs = lax.dynamic_slice_in_dim(station_pairs, facet * share, share, 1)
        observed = jnp.pad(observed, ((0, 0),) * 3 + ((0, pad),))
        station_pairs = jnp.pad(station_pairs, ((0, 0), (0, pad)), constant_values=-1)
    residual, part = pl.pallas_call(
        functools.partial(model_kernel, facets, sliced, cap),
        out_shape=(
            jax.ShapeDtypeStruct((2, 4, samples, width), f32),
            jax.ShapeDtypeStruct((facets, ROWS, stations // LANES, LANES), f32),
        ),
        in_specs=[smem, pl.BlockSpec(memory_space=pl.ANY), vmem, vmem, vmem],
        out_specs=(vmem, vmem),
        scratch_shapes=[
            pltpu.VMEM((32 + 8 * facets, stations), f32),
            pltpu.VMEM((2, 32 + 8 * facets, width), f32),
            pltpu.VMEM((2, stations, width), jnp.bfloat16),
            pltpu.VMEM((8, (TIMES + 1) * width), f32),
            pltpu.VMEM((cap, (TIMES + 1) * width), f32),
            pltpu.VMEM((facets, 2, samples, width), f32),
            pltpu.VMEM((2, 16 * facets, width), f32),
            pltpu.SemaphoreType.DMA,
        ],
        name="model_and_residual",
    )(facet.reshape(1), observed, station_pairs, jnp.transpose(station_uvw, (1, 0, 2)), params)
    if not sliced:
        residual = residual[..., :share]
    tile = (ROWS, stations // LANES, LANES)
    stages = radices(blocks)
    messages = facets - 1 + sum(r - 1 for r in stages)
    totals = pl.pallas_call(
        functools.partial(reduce_kernel, blocks, facets),
        out_shape=jax.ShapeDtypeStruct(tile, f32),
        in_specs=[vmem],
        out_specs=vmem,
        scratch_shapes=[pltpu.VMEM((len(stages),) + tile, f32), pltpu.VMEM((facets - 1,) + tile, f32)]
        + [pltpu.VMEM((r - 1,) + tile, f32) for r in stages]
        + [pltpu.SemaphoreType.DMA((messages,)), pltpu.SemaphoreType.DMA((messages,))],
        compiler_params=pltpu.CompilerParams(collective_id=1, has_side_effects=True),
        name="sum_stations",
    )(part)
    scaled = (totals[: ROWS - 1] / (jnp.sqrt(totals[ROWS - 1 :]) + 1.0)).reshape(2, 4, 1, stations)
    return residual, scaled


def solution(mesh):
    placed = (
        P(None, None, None, "base"),
        P(None, "base"),
        P(),
        P("facet", None, None),
        P("facet", None),
        P("facet"),
        P(None, None, "facet", None),
    )
    return jax.shard_map(
        functools.partial(body, mesh.shape["base"], mesh.shape["facet"]),
        mesh=mesh,
        in_specs=placed,
        out_specs=(P(None, None, None, ("base", "facet")), P(None, None, "facet", None)),
        check_vma=False,
    )
```

```python
import functools
import math

import jax
import jax.numpy as jnp
from jax import lax
from jax.experimental import pallas as pl
from jax.experimental.pallas import tpu as pltpu
from jax.sharding import PartitionSpec as P

MESH = pl.DeviceIdType.MESH
LANES = 128
TIMES = 4
CHANNELS = 16
ROWS = 9
STEP = 16
VMEM = pltpu.MemorySpace.VMEM
SMEM = pltpu.MemorySpace.SMEM

SIN = (4.442882919124344, -7.308245686509057, 3.6063542184328345, -0.846111650373896, 0.10982451642611356)
COS = (1.4142134962552284, -6.978850948563788, 5.73946037690675, -1.8835579059841707, 0.3106880275217573)


def poly(x, coefficients):
    value = coefficients[-1]
    for c in coefficients[-2::-1]:
        value = value * x + c
    return value


def cos_sin_turns(turns):
    magic = 12582912.0
    r = turns - ((turns + magic) - magic)
    x = r * r
    half_sin = r * poly(x, SIN)
    half_cos = poly(x, COS)
    return 1.0 - half_sin * half_sin, half_sin * half_cos


def split3(a):
    high = a.astype(jnp.bfloat16)
    rest = a - high.astype(jnp.float32)
    mid = rest.astype(jnp.bfloat16)
    low = (rest - mid.astype(jnp.float32)).astype(jnp.bfloat16)
    return high, mid, low


def exact_dot(a, hot, dims):
    out = None
    for part in split3(a):
        term = lax.dot_general(part, hot, (dims, ((), ())), preferred_element_type=jnp.float32)
        out = term if out is None else out + term
    return out


def product(a, b):
    out = []
    for i in range(2):
        for j in range(2):
            re = im = None
            for k in range(2):
                (x, y), (u, v) = a[2 * i + k], b[2 * k + j]
                r, s = x * u - y * v, x * v + y * u
                re, im = (r, s) if re is None else (re + r, im + s)
            out.append((re, im))
    return out


def adjoint(a):
    return [(a[i][0], -a[i][1]) for i in (0, 2, 1, 3)]


def radices(blocks):
    out = []
    while blocks > 1:
        out.append(4 if blocks % 4 == 0 else blocks)
        blocks //= out[-1]
    return out


def partners(blocks, facets):
    b = lax.axis_index("base")
    f = lax.axis_index("facet")
    phases = []
    stride = 1
    for radix in radices(blocks):
        digit = lax.rem(b // stride, radix)
        low = b - digit * stride
        turns = facets if stride == 1 else 1
        phases.append([(low + lax.rem(digit + d, radix) * stride, lax.rem(f + e, facets))
                       for d in range(radix) for e in range(turns) if d + e > 0])
        stride *= radix
    return phases


def message_counts(blocks, facets):
    return [r * (facets if i == 0 else 1) - 1 for i, r in enumerate(radices(blocks))]


def calibrate_kernel(blocks, facets, sliced, observed_ref, pairs_ref, uvw_ref, directions_ref, fluxes_ref, counts_ref,
                     gains_ref, out_ref, totals_ref, params, table, gathered, hot, base, angle, model, left, parts, mine,
                     *refs):
    phases = partners(blocks, facets)
    inboxes = refs[: len(phases)]
    copy_sem, params_send, params_recv, send_sem, recv_sem = refs[len(phases) :]
    me = lax.axis_index("facet")
    block = lax.axis_index("base")
    barrier = pltpu.get_barrier_semaphore()
    for phase in phases:
        for peer in phase:
            pl.semaphore_signal(barrier, inc=1, device_id=peer, device_id_type=MESH)
    width = out_ref.shape[3]
    stations = uvw_ref.shape[2]
    groups = stations // LANES
    cap = fluxes_ref.shape[1]
    start = pl.multiple_of(me * width, LANES)
    source = observed_ref.at[:, :, :, pl.ds(start, width)] if sliced else observed_ref
    copy = pltpu.make_async_copy(source, out_ref, copy_sem)
    copy.start()
    for i in range(2):
        for j in range(4):
            params[me, 4 * i + j : 4 * i + j + 1, :] = gains_ref[i, j]
    params[me, 8:16, :] = jnp.zeros((8, stations), jnp.float32)
    l = directions_ref[0, 0:1, :]
    m = directions_ref[0, 1:2, :]
    slots = lax.broadcasted_iota(jnp.int32, (1, cap), 1)
    params[me, 8:9, 0:cap] = l
    params[me, 9:10, 0:cap] = m
    params[me, 10:11, 0:cap] = jnp.sqrt(1.0 - l * l - m * m) - 1.0
    params[me, 11:12, 0:cap] = jnp.where(slots < counts_ref[0], fluxes_ref[...], 0.0)
    pairs = pairs_ref[:, pl.ds(start, width)] if sliced else pairs_ref[...]
    column = lax.broadcasted_iota(jnp.int32, (stations, width), 0)
    for side in range(2):
        hot[side] = (column == pairs[side : side + 1, :]).astype(jnp.float32).astype(jnp.bfloat16)
    pl.semaphore_wait(barrier, sum(message_counts(blocks, facets)))
    shares = []
    for d in range(1, facets):
        share = pltpu.make_async_remote_copy(
            src_ref=params.at[me], dst_ref=params.at[me], send_sem=params_send.at[d - 1],
            recv_sem=params_recv.at[d - 1], device_id=(block, lax.rem(me + d, facets)), device_id_type=MESH)
        share.start()
        shares.append(share)
    for t in range(TIMES):
        for axis in range(3):
            table[8 * t + axis : 8 * t + axis + 1, :] = uvw_ref[axis, t : t + 1, :]
        table[8 * t + 3 : 8 * t + 8, :] = jnp.zeros((5, stations), jnp.float32)
    table[32:40, :] = params[me, 0:8, :]
    own = pl.ds(pl.multiple_of(32 + 8 * me, 8), 8)
    for side in range(2):
        found = exact_dot(table[...], hot[side], ((1,), (0,)))
        gathered[side, 0:32, :] = found[0:32]
        gathered[side, own, :] = found[32:40]
    for t in range(TIMES):
        base[:, t * width : (t + 1) * width] = gathered[0, 8 * t : 8 * t + 8, :] - gathered[1, 8 * t : 8 * t + 8, :]
    row = lax.broadcasted_iota(jnp.int32, (8, width), 0)
    base[:, TIMES * width :] = (row == 3).astype(jnp.float32)

    def jones(k, side):
        rows = gathered[side, pl.ds(pl.multiple_of(32 + 8 * k, 8), 8), :]
        return [(rows[e : e + 1, :], rows[4 + e : 5 + e, :]) for e in range(4)]

    def facet_model(d, carry):
        k = lax.rem(me + d, facets)
        slots = jnp.transpose(params[k, 8:16, 0:cap])
        angle[...] = jnp.dot(slots, base[...], precision=lax.Precision.HIGHEST, preferred_element_type=jnp.float32)
        for t in range(TIMES):

            def step(i, acc):
                rows = pl.ds(pl.multiple_of(i * STEP, STEP), STEP)
                turns = angle[rows, t * width : (t + 1) * width]
                live = angle[rows, TIMES * width :]
                cz, sz = cos_sin_turns(turns * (79.0 / 64.0))
                c0, s0 = cos_sin_turns(turns * (1.0 / 64.0))
                cz, sz = cz * live, sz * live
                twice = 4.0 * (c0 * c0) - 2.0
                cs, ss = [c0, (twice - 1.0) * c0], [s0, (twice + 1.0) * s0]
                for j in range(2):
                    cs.append(twice * cs[-1] - cs[-2])
                    ss.append(twice * ss[-1] - ss[-2])
                c4 = cs[3] * c0 - ss[3] * s0
                s4 = ss[3] * c0 + cs[3] * s0
                cc, sn, sc, cn = cz * c4, sz * s4, sz * c4, cz * s4
                centres = ((cc + sn, sc - cn), (cc - sn, sc + cn))
                out = []
                for a, b in centres:
                    for j in range(4):
                        for value in (a * cs[j], b * ss[j], a * ss[j], b * cs[j]):
                            out.append(acc[len(out)] + (value[0:8] + value[8:16]))
                return tuple(out)

            zero = jnp.zeros((8, width), jnp.float32)
            acc = lax.fori_loop(0, cap // STEP, step, (zero,) * 32)
            real, imaginary = [None] * CHANNELS, [None] * CHANNELS
            for centre in range(2):
                for j in range(4):
                    p = acc[16 * centre + 4 * j : 16 * centre + 4 * j + 4]
                    up, down = 8 * centre + 4 + j, 8 * centre + 3 - j
                    real[up], real[down] = p[0] - p[1], p[0] + p[1]
                    imaginary[up], imaginary[down] = -(p[2] + p[3]), p[2] - p[3]
            for part, values in enumerate((real, imaginary)):
                sums = [jnp.sum(v, axis=0, keepdims=True) for v in values]
                model[k, part, CHANNELS * t : CHANNELS * (t + 1), :] = jnp.concatenate(sums, axis=0)
        return carry

    facet_model(0, 0)
    for d, share in enumerate(shares, 1):
        other = lax.rem(me + facets - d, facets)
        pltpu.make_async_copy(params.at[other], params.at[other], params_recv.at[d - 1]).wait()
        rows = pl.ds(pl.multiple_of(32 + 8 * other, 8), 8)
        for side in range(2):
            gathered[side, rows, :] = exact_dot(params[other, 0:8, :], hot[side], ((1,), (0,)))
    lax.fori_loop(1, facets, facet_model, 0)
    copy.wait()

    def subtract(k, carry):
        prod = product(jones(k, 0), adjoint(jones(k, 1)))
        re, im = model[k, 0], model[k, 1]
        for e, (x, y) in enumerate(prod):
            out_ref[0, e] = out_ref[0, e] - (re * x - im * y)
            out_ref[1, e] = out_ref[1, e] - (re * y + im * x)
        return carry

    lax.fori_loop(0, facets, subtract, 0)

    def terms(k, carry):
        re, im = model[k, 0], model[k, 1]
        acc = []
        for e in range(4):
            x, y = out_ref[0, e], out_ref[1, e]
            acc.append((jnp.sum(re * x + im * y, axis=0, keepdims=True), jnp.sum(re * y - im * x, axis=0, keepdims=True)))
        power = jnp.sum(re * re + im * im, axis=0, keepdims=True)
        first, second = jones(k, 0), jones(k, 1)
        for side, (grad, other) in enumerate(((product(acc, second), second), (product(adjoint(acc), first), first))):
            norm = None
            for x, y in other:
                norm = x * x + y * y if norm is None else norm + (x * x + y * y)
            rows = [-grad[e][0] for e in range(4)] + [-grad[e][1] for e in range(4)] + [power * norm]
            left[side, pl.ds(pl.multiple_of(16 * k, 16), 16), :] = jnp.concatenate(
                rows + [jnp.zeros((7, width), jnp.float32)], axis=0)
        return carry

    lax.fori_loop(0, facets, terms, 0)
    sums = None
    for side in range(2):
        term = exact_dot(left[side], hot[side], ((1,), (1,)))
        sums = term if sums is None else sums + term
    for k in range(facets):
        for r in range(ROWS):
            for g in range(groups):
                parts[k, r, g : g + 1, :] = sums[16 * k + r : 16 * k + r + 1, g * LANES : (g + 1) * LANES]
    value = parts[me]
    copies = []
    for s, (phase, inbox) in enumerate(zip(phases, inboxes)):
        if s > 0:
            mine[s - 1] = value
        before = len(copies)
        for d, peer in enumerate(phase):
            message = pltpu.make_async_remote_copy(
                src_ref=parts.at[peer[1]] if s == 0 else mine.at[s - 1], dst_ref=inbox.at[d],
                send_sem=send_sem.at[before + d], recv_sem=recv_sem.at[before + d], device_id=peer, device_id_type=MESH)
            message.start()
            copies.append(message)
        for message in copies[before:]:
            message.wait_recv()
        for d in range(len(phase)):
            value = value + inbox[d]
    totals_ref[...] = value
    for message in copies + shares:
        message.wait_send()


def body(blocks, facets, observed, station_pairs, station_uvw, directions, fluxes, counts, jones_gains):
    f32 = jnp.float32
    stations = jones_gains.shape[3]
    cap = fluxes.shape[1]
    samples = observed.shape[2]
    share = observed.shape[3] // facets
    vmem = pl.BlockSpec(memory_space=VMEM)
    smem = pl.BlockSpec(memory_space=SMEM)
    facet = lax.axis_index("facet")
    width = -(-share // LANES) * LANES
    sliced = width == share
    if not sliced:
        pad = width - share
        observed = lax.dynamic_slice_in_dim(observed, facet * share, share, 3)
        station_pairs = lax.dynamic_slice_in_dim(station_pairs, facet * share, share, 1)
        observed = jnp.pad(observed, ((0, 0),) * 3 + ((0, pad),))
        station_pairs = jnp.pad(station_pairs, ((0, 0), (0, pad)), constant_values=-1)
    tile = (ROWS, stations // LANES, LANES)
    messages = message_counts(blocks, facets)
    dma = pltpu.SemaphoreType.DMA
    residual, totals = pl.pallas_call(
        functools.partial(calibrate_kernel, blocks, facets, sliced),
        out_shape=(jax.ShapeDtypeStruct((2, 4, samples, width), f32), jax.ShapeDtypeStruct(tile, f32)),
        in_specs=[pl.BlockSpec(memory_space=pl.ANY), vmem, vmem, vmem, vmem, smem, vmem],
        out_specs=(vmem, vmem),
        scratch_shapes=[
            pltpu.VMEM((facets, 16, stations), f32),
            pltpu.VMEM((40, stations), f32),
            pltpu.VMEM((2, 32 + 8 * facets, width), f32),
            pltpu.VMEM((2, stations, width), jnp.bfloat16),
            pltpu.VMEM((8, (TIMES + 1) * width), f32),
            pltpu.VMEM((cap, (TIMES + 1) * width), f32),
            pltpu.VMEM((facets, 2, samples, width), f32),
            pltpu.VMEM((2, 16 * facets, width), f32),
            pltpu.VMEM((facets,) + tile, f32),
            pltpu.VMEM((max(len(messages) - 1, 1),) + tile, f32),
        ]
        + [pltpu.VMEM((n,) + tile, f32) for n in messages]
        + [dma, dma((facets - 1,)), dma((facets - 1,)), dma((sum(messages),)), dma((sum(messages),))],
        compiler_params=pltpu.CompilerParams(collective_id=0, has_side_effects=True),
        name="calibrate",
    )(observed, station_pairs, jnp.transpose(station_uvw, (1, 0, 2)), directions, fluxes, counts, jones_gains)
    if not sliced:
        residual = residual[..., :share]
    scaled = (totals[: ROWS - 1] / (jnp.sqrt(totals[ROWS - 1 :]) + 1.0)).reshape(2, 4, 1, stations)
    return residual, scaled


def solution(mesh):
    placed = (
        P(None, None, None, "base"),
        P(None, "base"),
        P(),
        P("facet", None, None),
        P("facet", None),
        P("facet"),
        P(None, None, "facet", None),
    )
    return jax.shard_map(
        functools.partial(body, mesh.shape["base"], mesh.shape["facet"]),
        mesh=mesh,
        in_specs=placed,
        out_specs=(P(None, None, None, ("base", "facet")), P(None, None, "facet", None)),
        check_vma=False,
    )
```

```python
import functools
import math

import jax
import jax.numpy as jnp
from jax import lax
from jax.experimental import pallas as pl
from jax.experimental.pallas import tpu as pltpu
from jax.sharding import PartitionSpec as P

MESH = pl.DeviceIdType.MESH
LANES = 128
TIMES = 4
CHANNELS = 16
ROWS = 9
STEP = 16
VMEM = pltpu.MemorySpace.VMEM
SMEM = pltpu.MemorySpace.SMEM

SIN = (4.442882919124344, -7.308245686509057, 3.6063542184328345, -0.846111650373896, 0.10982451642611356)
COS = (1.4142134962552284, -6.978850948563788, 5.73946037690675, -1.8835579059841707, 0.3106880275217573)


def poly(x, coefficients):
    value = coefficients[-1]
    for c in coefficients[-2::-1]:
        value = value * x + c
    return value


def cos_sin_turns(turns):
    magic = 12582912.0
    r = turns - ((turns + magic) - magic)
    x = r * r
    half_sin = r * poly(x, SIN)
    half_cos = poly(x, COS)
    return 1.0 - half_sin * half_sin, half_sin * half_cos


def split3(a):
    high = a.astype(jnp.bfloat16)
    rest = a - high.astype(jnp.float32)
    mid = rest.astype(jnp.bfloat16)
    low = (rest - mid.astype(jnp.float32)).astype(jnp.bfloat16)
    return high, mid, low


def exact_dot(a, hot, dims):
    rows = a.shape[0]
    out = lax.dot_general(jnp.concatenate(split3(a), axis=0), hot, (dims, ((), ())), preferred_element_type=jnp.float32)
    return out[:rows] + out[rows : 2 * rows] + out[2 * rows :]


def product(a, b):
    out = []
    for i in range(2):
        for j in range(2):
            re = im = None
            for k in range(2):
                (x, y), (u, v) = a[2 * i + k], b[2 * k + j]
                r, s = x * u - y * v, x * v + y * u
                re, im = (r, s) if re is None else (re + r, im + s)
            out.append((re, im))
    return out


def adjoint(a):
    return [(a[i][0], -a[i][1]) for i in (0, 2, 1, 3)]


def radices(blocks):
    out = []
    while blocks > 1:
        out.append(4 if blocks % 4 == 0 else blocks)
        blocks //= out[-1]
    return out


def partners(blocks, facets):
    b = lax.axis_index("base")
    f = lax.axis_index("facet")
    phases = []
    stride = 1
    for radix in radices(blocks):
        digit = lax.rem(b // stride, radix)
        low = b - digit * stride
        turns = facets if stride == 1 else 1
        phases.append([(low + lax.rem(digit + d, radix) * stride, lax.rem(f + e, facets))
                       for d in range(radix) for e in range(turns) if d + e > 0])
        stride *= radix
    return phases


def message_counts(blocks, facets):
    return [r * (facets if i == 0 else 1) - 1 for i, r in enumerate(radices(blocks))]


def calibrate_kernel(blocks, facets, sliced, observed_ref, pairs_ref, uvw_ref, directions_ref, fluxes_ref, counts_ref,
                     gains_ref, residual_ref, totals_ref, out_ref, params, table, gathered, hot, base, angle, model, left, parts, mine,
                     *refs):
    phases = partners(blocks, facets)
    inboxes = refs[: len(phases)]
    copy_sem, out_sem, params_send, params_recv, send_sem, recv_sem = refs[len(phases) :]
    me = lax.axis_index("facet")
    block = lax.axis_index("base")
    barrier = pltpu.get_barrier_semaphore()
    for phase in phases:
        for peer in phase:
            pl.semaphore_signal(barrier, inc=1, device_id=peer, device_id_type=MESH)
    width = out_ref.shape[3]
    stations = uvw_ref.shape[2]
    groups = stations // LANES
    cap = fluxes_ref.shape[1]
    start = pl.multiple_of(me * width, LANES)
    source = observed_ref.at[:, :, :, pl.ds(start, width)] if sliced else observed_ref
    copy = pltpu.make_async_copy(source, out_ref, copy_sem)
    copy.start()
    for i in range(2):
        for j in range(4):
            params[me, 4 * i + j : 4 * i + j + 1, :] = gains_ref[i, j]
    params[me, 8:16, :] = jnp.zeros((8, stations), jnp.float32)
    l = directions_ref[0, 0:1, :]
    m = directions_ref[0, 1:2, :]
    slots = lax.broadcasted_iota(jnp.int32, (1, cap), 1)
    params[me, 8:9, 0:cap] = l
    params[me, 9:10, 0:cap] = m
    params[me, 10:11, 0:cap] = jnp.sqrt(1.0 - l * l - m * m) - 1.0
    params[me, 11:12, 0:cap] = jnp.where(slots < counts_ref[0], fluxes_ref[...], 0.0)
    pairs = pairs_ref[:, pl.ds(start, width)] if sliced else pairs_ref[...]
    column = lax.broadcasted_iota(jnp.int32, (stations, width), 0)
    for side in range(2):
        hot[side] = (column == pairs[side : side + 1, :]).astype(jnp.float32).astype(jnp.bfloat16)
    pl.semaphore_wait(barrier, sum(message_counts(blocks, facets)))
    shares = []
    for d in range(1, facets):
        share = pltpu.make_async_remote_copy(
            src_ref=params.at[me], dst_ref=params.at[me], send_sem=params_send.at[d - 1],
            recv_sem=params_recv.at[d - 1], device_id=(block, lax.rem(me + d, facets)), device_id_type=MESH)
        share.start()
        shares.append(share)
    for t in range(TIMES):
        for axis in range(3):
            table[8 * t + axis : 8 * t + axis + 1, :] = uvw_ref[axis, t : t + 1, :]
        table[8 * t + 3 : 8 * t + 8, :] = jnp.zeros((5, stations), jnp.float32)
    table[32:48, :] = params[me]
    own = pl.ds(pl.multiple_of(32 + 8 * me, 8), 8)
    for side in range(2):
        found = exact_dot(table[...], hot[side], ((1,), (0,)))
        gathered[side, 0:32, :] = found[0:32]
        gathered[side, own, :] = found[32:40]
    for t in range(TIMES):
        base[:, t * width : (t + 1) * width] = gathered[0, 8 * t : 8 * t + 8, :] - gathered[1, 8 * t : 8 * t + 8, :]

    def jones(k, side):
        rows = gathered[side, pl.ds(pl.multiple_of(32 + 8 * k, 8), 8), :]
        return [(rows[e : e + 1, :], rows[4 + e : 5 + e, :]) for e in range(4)]

    def facet_model(d, carry):
        k = lax.rem(me + d, facets)
        slots = jnp.transpose(params[k, 8:16, 0:cap])
        for v in range(4):
            angle[v] = jnp.broadcast_to(slots[:, v : v + 1], (cap, width))
        for t in range(TIMES):
            u, v, w = (jnp.broadcast_to(base[c : c + 1, t * width : (t + 1) * width], (STEP, width)) for c in range(3))

            def step(i, acc, u=u, v=v, w=w):
                rows = pl.ds(pl.multiple_of(i * STEP, STEP), STEP)
                turns = u * angle[0, rows, :] + v * angle[1, rows, :] + w * angle[2, rows, :]
                live = angle[3, rows, :]
                cz, sz = cos_sin_turns(turns * (79.0 / 64.0))
                c0, s0 = cos_sin_turns(turns * (1.0 / 64.0))
                cz, sz = cz * live, sz * live
                twice = 4.0 * (c0 * c0) - 2.0
                cs, ss = [c0, (twice - 1.0) * c0], [s0, (twice + 1.0) * s0]
                for j in range(2):
                    cs.append(twice * cs[-1] - cs[-2])
                    ss.append(twice * ss[-1] - ss[-2])
                c4 = cs[3] * c0 - ss[3] * s0
                s4 = ss[3] * c0 + cs[3] * s0
                cc, sn, sc, cn = cz * c4, sz * s4, sz * c4, cz * s4
                centres = ((cc + sn, sc - cn), (cc - sn, sc + cn))
                out = []
                for a, b in centres:
                    for j in range(4):
                        for value in (a * cs[j], b * ss[j], a * ss[j], b * cs[j]):
                            out.append(acc[len(out)] + (value[0:8] + value[8:16]))
                return tuple(out)

            zero = jnp.zeros((8, width), jnp.float32)
            acc = lax.fori_loop(0, cap // STEP, step, (zero,) * 32, unroll=4)
            real, imaginary = [None] * CHANNELS, [None] * CHANNELS
            for centre in range(2):
                for j in range(4):
                    p = acc[16 * centre + 4 * j : 16 * centre + 4 * j + 4]
                    up, down = 8 * centre + 4 + j, 8 * centre + 3 - j
                    real[up], real[down] = p[0] - p[1], p[0] + p[1]
                    imaginary[up], imaginary[down] = -(p[2] + p[3]), p[2] - p[3]
            for part, values in enumerate((real, imaginary)):
                sums = [jnp.sum(v, axis=0, keepdims=True) for v in values]
                model[k, part, CHANNELS * t : CHANNELS * (t + 1), :] = jnp.concatenate(sums, axis=0)
        return carry

    facet_model(0, 0)
    for d, share in enumerate(shares, 1):
        other = lax.rem(me + facets - d, facets)
        pltpu.make_async_copy(params.at[other], params.at[other], params_recv.at[d - 1]).wait()
        rows = pl.ds(pl.multiple_of(32 + 8 * other, 8), 8)
        for side in range(2):
            gathered[side, rows, :] = exact_dot(params[other], hot[side], ((1,), (0,)))[0:8]
    lax.fori_loop(1, facets, facet_model, 0)
    copy.wait()

    def subtract(k, carry):
        prod = product(jones(k, 0), adjoint(jones(k, 1)))
        re, im = model[k, 0], model[k, 1]
        for e, (x, y) in enumerate(prod):
            out_ref[0, e] = out_ref[0, e] - (re * x - im * y)
            out_ref[1, e] = out_ref[1, e] - (re * y + im * x)
        return carry

    lax.fori_loop(0, facets, subtract, 0)
    written = pltpu.make_async_copy(out_ref, residual_ref, out_sem)
    written.start()

    def terms(k, carry):
        re, im = model[k, 0], model[k, 1]
        acc = []
        for e in range(4):
            x, y = out_ref[0, e], out_ref[1, e]
            acc.append((jnp.sum(re * x + im * y, axis=0, keepdims=True), jnp.sum(re * y - im * x, axis=0, keepdims=True)))
        power = jnp.sum(re * re + im * im, axis=0, keepdims=True)
        first, second = jones(k, 0), jones(k, 1)
        for side, (grad, other) in enumerate(((product(acc, second), second), (product(adjoint(acc), first), first))):
            norm = None
            for x, y in other:
                norm = x * x + y * y if norm is None else norm + (x * x + y * y)
            rows = [-grad[e][0] for e in range(4)] + [-grad[e][1] for e in range(4)] + [power * norm]
            left[side, pl.ds(pl.multiple_of(16 * k, 16), 16), :] = jnp.concatenate(
                rows + [jnp.zeros((7, width), jnp.float32)], axis=0)
        return carry

    lax.fori_loop(0, facets, terms, 0)
    sums = None
    for side in range(2):
        term = exact_dot(left[side], hot[side], ((1,), (1,)))
        sums = term if sums is None else sums + term
    for k in range(facets):
        for r in range(ROWS):
            for g in range(groups):
                parts[k, r, g : g + 1, :] = sums[16 * k + r : 16 * k + r + 1, g * LANES : (g + 1) * LANES]
    value = parts[me]
    copies = []
    for s, (phase, inbox) in enumerate(zip(phases, inboxes)):
        if s > 0:
            mine[s - 1] = value
        before = len(copies)
        for d, peer in enumerate(phase):
            message = pltpu.make_async_remote_copy(
                src_ref=parts.at[peer[1]] if s == 0 else mine.at[s - 1], dst_ref=inbox.at[d],
                send_sem=send_sem.at[before + d], recv_sem=recv_sem.at[before + d], device_id=peer, device_id_type=MESH)
            message.start()
            copies.append(message)
        for message in copies[before:]:
            message.wait_recv()
        for d in range(len(phase)):
            value = value + inbox[d]
    totals_ref[...] = value
    for message in copies + shares:
        message.wait_send()
    written.wait()


def finish_kernel(totals_ref, residual_ref, scaled_ref, out_ref, copy_sem):
    copy = pltpu.make_async_copy(residual_ref, out_ref, copy_sem)
    copy.start()
    scale = 1.0 / (jnp.sqrt(totals_ref[ROWS - 1]) + 1.0)
    for r in range(ROWS - 1):
        value = totals_ref[r] * scale
        for g in range(value.shape[0]):
            scaled_ref[r // 4, r % 4, 0:1, g * LANES : (g + 1) * LANES] = value[g : g + 1, :]
    copy.wait()


def body(blocks, facets, observed, station_pairs, station_uvw, directions, fluxes, counts, jones_gains):
    f32 = jnp.float32
    stations = jones_gains.shape[3]
    cap = fluxes.shape[1]
    samples = observed.shape[2]
    share = observed.shape[3] // facets
    vmem = pl.BlockSpec(memory_space=VMEM)
    smem = pl.BlockSpec(memory_space=SMEM)
    facet = lax.axis_index("facet")
    width = -(-share // LANES) * LANES
    sliced = width == share
    if not sliced:
        pad = width - share
        observed = lax.dynamic_slice_in_dim(observed, facet * share, share, 3)
        station_pairs = lax.dynamic_slice_in_dim(station_pairs, facet * share, share, 1)
        observed = jnp.pad(observed, ((0, 0),) * 3 + ((0, pad),))
        station_pairs = jnp.pad(station_pairs, ((0, 0), (0, pad)), constant_values=-1)
    tile = (ROWS, stations // LANES, LANES)
    messages = message_counts(blocks, facets)
    dma = pltpu.SemaphoreType.DMA
    residual, totals = pl.pallas_call(
        functools.partial(calibrate_kernel, blocks, facets, sliced),
        out_shape=(jax.ShapeDtypeStruct((2, 4, samples, width), f32), jax.ShapeDtypeStruct(tile, f32)),
        in_specs=[pl.BlockSpec(memory_space=pl.ANY), vmem, vmem, vmem, vmem, smem, vmem],
        out_specs=(pl.BlockSpec(memory_space=pl.ANY), vmem),
        scratch_shapes=[
            pltpu.VMEM((2, 4, samples, width), f32),
            pltpu.VMEM((facets, 16, stations), f32),
            pltpu.VMEM((48, stations), f32),
            pltpu.VMEM((2, 32 + 8 * facets, width), f32),
            pltpu.VMEM((2, stations, width), jnp.bfloat16),
            pltpu.VMEM((8, TIMES * width), f32),
            pltpu.VMEM((4, cap, width), f32),
            pltpu.VMEM((facets, 2, samples, width), f32),
            pltpu.VMEM((2, 16 * facets, width), f32),
            pltpu.VMEM((facets,) + tile, f32),
            pltpu.VMEM((max(len(messages) - 1, 1),) + tile, f32),
        ]
        + [pltpu.VMEM((n,) + tile, f32) for n in messages]
        + [dma, dma, dma((facets - 1,)), dma((facets - 1,)), dma((sum(messages),)), dma((sum(messages),))],
        compiler_params=pltpu.CompilerParams(collective_id=0, has_side_effects=True),
        name="calibrate",
    )(observed, station_pairs, jnp.transpose(station_uvw, (1, 0, 2)), directions, fluxes, counts, jones_gains)
    anywhere = pl.BlockSpec(memory_space=pl.ANY)
    scaled, residual = pl.pallas_call(
        finish_kernel,
        out_shape=(jax.ShapeDtypeStruct((2, 4, 1, stations), f32), jax.ShapeDtypeStruct(residual.shape, f32)),
        in_specs=[vmem, anywhere],
        out_specs=(vmem, vmem),
        scratch_shapes=[dma],
        name="finish",
    )(totals, residual)
    if not sliced:
        residual = residual[..., :share]
    return residual, scaled


def solution(mesh):
    placed = (
        P(None, None, None, "base"),
        P(None, "base"),
        P(),
        P("facet", None, None),
        P("facet", None),
        P("facet"),
        P(None, None, "facet", None),
    )
    return jax.shard_map(
        functools.partial(body, mesh.shape["base"], mesh.shape["facet"]),
        mesh=mesh,
        in_specs=placed,
        out_specs=(P(None, None, None, ("base", "facet")), P(None, None, "facet", None)),
        check_vma=False,
    )
```

```python
import functools
import math

import jax
import jax.numpy as jnp
from jax import lax
from jax.experimental import pallas as pl
from jax.experimental.pallas import tpu as pltpu
from jax.sharding import PartitionSpec as P

MESH = pl.DeviceIdType.MESH
LANES = 128
TIMES = 4
CHANNELS = 16
ROWS = 9
STEP = 16
VMEM = pltpu.MemorySpace.VMEM
SMEM = pltpu.MemorySpace.SMEM

SIN = (4.442882919124344, -7.308245686509057, 3.6063542184328345, -0.846111650373896, 0.10982451642611356)
COS = (1.4142134962552284, -6.978850948563788, 5.73946037690675, -1.8835579059841707, 0.3106880275217573)


def poly(x, coefficients):
    value = coefficients[-1]
    for c in coefficients[-2::-1]:
        value = value * x + c
    return value


def cos_sin_turns(turns):
    magic = 12582912.0
    r = turns - ((turns + magic) - magic)
    x = r * r
    half_sin = r * poly(x, SIN)
    half_cos = poly(x, COS)
    return 1.0 - half_sin * half_sin, half_sin * half_cos


def split3(a):
    high = a.astype(jnp.bfloat16)
    rest = a - high.astype(jnp.float32)
    mid = rest.astype(jnp.bfloat16)
    low = (rest - mid.astype(jnp.float32)).astype(jnp.bfloat16)
    return high, mid, low


def exact_dot(a, hot, dims):
    rows = a.shape[0]
    out = lax.dot_general(jnp.concatenate(split3(a), axis=0), hot, (dims, ((), ())), preferred_element_type=jnp.float32)
    return out[:rows] + out[rows : 2 * rows] + out[2 * rows :]


def product(a, b):
    out = []
    for i in range(2):
        for j in range(2):
            re = im = None
            for k in range(2):
                (x, y), (u, v) = a[2 * i + k], b[2 * k + j]
                r, s = x * u - y * v, x * v + y * u
                re, im = (r, s) if re is None else (re + r, im + s)
            out.append((re, im))
    return out


def adjoint(a):
    return [(a[i][0], -a[i][1]) for i in (0, 2, 1, 3)]


def radices(blocks):
    out = []
    while blocks > 1:
        out.append(4 if blocks % 4 == 0 else blocks)
        blocks //= out[-1]
    return out


def partners(blocks, facets):
    b = lax.axis_index("base")
    f = lax.axis_index("facet")
    phases = []
    stride = 1
    for radix in radices(blocks):
        digit = lax.rem(b // stride, radix)
        low = b - digit * stride
        turns = facets if stride == 1 else 1
        phases.append([(low + lax.rem(digit + d, radix) * stride, lax.rem(f + e, facets))
                       for d in range(radix) for e in range(turns) if d + e > 0])
        stride *= radix
    return phases


def message_counts(blocks, facets):
    return [r * (facets if i == 0 else 1) - 1 for i, r in enumerate(radices(blocks))]


def calibrate_kernel(blocks, facets, sliced, observed_ref, pairs_ref, uvw_ref, directions_ref, fluxes_ref, counts_ref,
                     gains_ref, residual_ref, totals_ref, out_ref, params, table, gathered, hot, base, angle, model, left, parts, mine,
                     *refs):
    phases = partners(blocks, facets)
    inboxes = refs[: len(phases)]
    copy_sem, out_sem, params_send, params_recv, send_sem, recv_sem = refs[len(phases) :]
    me = lax.axis_index("facet")
    block = lax.axis_index("base")
    barrier = pltpu.get_barrier_semaphore()
    for phase in phases:
        for peer in phase:
            pl.semaphore_signal(barrier, inc=1, device_id=peer, device_id_type=MESH)
    width = out_ref.shape[3]
    stations = uvw_ref.shape[2]
    groups = stations // LANES
    cap = fluxes_ref.shape[1]
    start = pl.multiple_of(me * width, LANES)
    source = observed_ref.at[:, :, :, pl.ds(start, width)] if sliced else observed_ref
    copy = pltpu.make_async_copy(source, out_ref, copy_sem)
    copy.start()
    for i in range(2):
        for j in range(4):
            params[me, 4 * i + j : 4 * i + j + 1, :] = gains_ref[i, j]
    params[me, 8:16, :] = jnp.zeros((8, stations), jnp.float32)
    l = directions_ref[0, 0:1, :]
    m = directions_ref[0, 1:2, :]
    slots = lax.broadcasted_iota(jnp.int32, (1, cap), 1)
    params[me, 8:9, 0:cap] = l
    params[me, 9:10, 0:cap] = m
    params[me, 10:11, 0:cap] = jnp.sqrt(1.0 - l * l - m * m) - 1.0
    params[me, 11:12, 0:cap] = jnp.where(slots < counts_ref[0], fluxes_ref[...], 0.0)
    pairs = pairs_ref[:, pl.ds(start, width)] if sliced else pairs_ref[...]
    column = lax.broadcasted_iota(jnp.int32, (stations, width), 0)
    for side in range(2):
        hot[side] = (column == pairs[side : side + 1, :]).astype(jnp.float32).astype(jnp.bfloat16)
    pl.semaphore_wait(barrier, sum(message_counts(blocks, facets)))
    shares = []
    for d in range(1, facets):
        share = pltpu.make_async_remote_copy(
            src_ref=params.at[me], dst_ref=params.at[me], send_sem=params_send.at[d - 1],
            recv_sem=params_recv.at[d - 1], device_id=(block, lax.rem(me + d, facets)), device_id_type=MESH)
        share.start()
        shares.append(share)
    for t in range(TIMES):
        for axis in range(3):
            table[8 * t + axis : 8 * t + axis + 1, :] = uvw_ref[axis, t : t + 1, :]
        table[8 * t + 3 : 8 * t + 8, :] = jnp.zeros((5, stations), jnp.float32)
    table[32:48, :] = params[me]
    own = pl.ds(pl.multiple_of(32 + 8 * me, 8), 8)
    for side in range(2):
        found = exact_dot(table[...], hot[side], ((1,), (0,)))
        gathered[side, 0:32, :] = found[0:32]
        gathered[side, own, :] = found[32:40]
    for t in range(TIMES):
        base[:, t * width : (t + 1) * width] = gathered[0, 8 * t : 8 * t + 8, :] - gathered[1, 8 * t : 8 * t + 8, :]

    def jones(k, side):
        rows = gathered[side, pl.ds(pl.multiple_of(32 + 8 * k, 8), 8), :]
        return [(rows[e : e + 1, :], rows[4 + e : 5 + e, :]) for e in range(4)]

    def facet_model(d, carry):
        k = lax.rem(me + d, facets)
        slots = jnp.transpose(params[k, 8:16, 0:cap])
        for v in range(4):
            angle[v] = jnp.broadcast_to(slots[:, v : v + 1], (cap, width))
        for t in range(TIMES):
            u, v, w = (jnp.broadcast_to(base[c : c + 1, t * width : (t + 1) * width], (STEP, width)) for c in range(3))

            def step(i, acc, u=u, v=v, w=w):
                rows = pl.ds(pl.multiple_of(i * STEP, STEP), STEP)
                turns = u * angle[0, rows, :] + v * angle[1, rows, :] + w * angle[2, rows, :]
                live = angle[3, rows, :]
                cz, sz = cos_sin_turns(turns * (79.0 / 64.0))
                c0, s0 = cos_sin_turns(turns * (1.0 / 64.0))
                cz, sz = cz * live, sz * live
                twice = 4.0 * (c0 * c0) - 2.0
                cs, ss = [c0, (twice - 1.0) * c0], [s0, (twice + 1.0) * s0]
                for j in range(2):
                    cs.append(twice * cs[-1] - cs[-2])
                    ss.append(twice * ss[-1] - ss[-2])
                c4 = cs[3] * c0 - ss[3] * s0
                s4 = ss[3] * c0 + cs[3] * s0
                cc, sn, sc, cn = cz * c4, sz * s4, sz * c4, cz * s4
                centres = ((cc + sn, sc - cn), (cc - sn, sc + cn))
                out = []
                for a, b in centres:
                    for j in range(4):
                        for value in (a * cs[j], b * ss[j], a * ss[j], b * cs[j]):
                            out.append(acc[len(out)] + (value[0:8] + value[8:16]))
                return tuple(out)

            zero = jnp.zeros((8, width), jnp.float32)
            acc = lax.fori_loop(0, cap // STEP, step, (zero,) * 32, unroll=8)
            real, imaginary = [None] * CHANNELS, [None] * CHANNELS
            for centre in range(2):
                for j in range(4):
                    p = acc[16 * centre + 4 * j : 16 * centre + 4 * j + 4]
                    up, down = 8 * centre + 4 + j, 8 * centre + 3 - j
                    real[up], real[down] = p[0] - p[1], p[0] + p[1]
                    imaginary[up], imaginary[down] = -(p[2] + p[3]), p[2] - p[3]
            for part, values in enumerate((real, imaginary)):
                sums = [jnp.sum(v, axis=0, keepdims=True) for v in values]
                model[k, part, CHANNELS * t : CHANNELS * (t + 1), :] = jnp.concatenate(sums, axis=0)
        return carry

    facet_model(0, 0)
    for d, share in enumerate(shares, 1):
        other = lax.rem(me + facets - d, facets)
        pltpu.make_async_copy(params.at[other], params.at[other], params_recv.at[d - 1]).wait()
        rows = pl.ds(pl.multiple_of(32 + 8 * other, 8), 8)
        for side in range(2):
            gathered[side, rows, :] = exact_dot(params[other], hot[side], ((1,), (0,)))[0:8]
    lax.fori_loop(1, facets, facet_model, 0)
    copy.wait()

    def subtract(k, carry):
        prod = product(jones(k, 0), adjoint(jones(k, 1)))
        re, im = model[k, 0], model[k, 1]
        for e, (x, y) in enumerate(prod):
            out_ref[0, e] = out_ref[0, e] - (re * x - im * y)
            out_ref[1, e] = out_ref[1, e] - (re * y + im * x)
        return carry

    lax.fori_loop(0, facets, subtract, 0, unroll=2)
    written = pltpu.make_async_copy(out_ref, residual_ref, out_sem)
    written.start()

    def terms(k, carry):
        re, im = model[k, 0], model[k, 1]
        acc = []
        for e in range(4):
            x, y = out_ref[0, e], out_ref[1, e]
            acc.append((jnp.sum(re * x + im * y, axis=0, keepdims=True), jnp.sum(re * y - im * x, axis=0, keepdims=True)))
        power = jnp.sum(re * re + im * im, axis=0, keepdims=True)
        first, second = jones(k, 0), jones(k, 1)
        for side, (grad, other) in enumerate(((product(acc, second), second), (product(adjoint(acc), first), first))):
            norm = None
            for x, y in other:
                norm = x * x + y * y if norm is None else norm + (x * x + y * y)
            rows = [-grad[e][0] for e in range(4)] + [-grad[e][1] for e in range(4)] + [power * norm]
            left[side, pl.ds(pl.multiple_of(16 * k, 16), 16), :] = jnp.concatenate(
                rows + [jnp.zeros((7, width), jnp.float32)], axis=0)
        return carry

    lax.fori_loop(0, facets, terms, 0, unroll=2)
    sums = None
    for side in range(2):
        term = exact_dot(left[side], hot[side], ((1,), (1,)))
        sums = term if sums is None else sums + term
    for k in range(facets):
        for r in range(ROWS):
            for g in range(groups):
                parts[k, r, g : g + 1, :] = sums[16 * k + r : 16 * k + r + 1, g * LANES : (g + 1) * LANES]
    value = parts[me]
    copies = []
    for s, (phase, inbox) in enumerate(zip(phases, inboxes)):
        if s > 0:
            mine[s - 1] = value
        before = len(copies)
        for d, peer in enumerate(phase):
            message = pltpu.make_async_remote_copy(
                src_ref=parts.at[peer[1]] if s == 0 else mine.at[s - 1], dst_ref=inbox.at[d],
                send_sem=send_sem.at[before + d], recv_sem=recv_sem.at[before + d], device_id=peer, device_id_type=MESH)
            message.start()
            copies.append(message)
        for message in copies[before:]:
            message.wait_recv()
        for d in range(len(phase)):
            value = value + inbox[d]
    totals_ref[...] = value
    for message in copies + shares:
        message.wait_send()
    written.wait()


def finish_kernel(totals_ref, residual_ref, scaled_ref, out_ref, copy_sem):
    copy = pltpu.make_async_copy(residual_ref, out_ref, copy_sem)
    copy.start()
    scale = 1.0 / (jnp.sqrt(totals_ref[ROWS - 1]) + 1.0)
    for r in range(ROWS - 1):
        value = totals_ref[r] * scale
        for g in range(value.shape[0]):
            scaled_ref[r // 4, r % 4, 0:1, g * LANES : (g + 1) * LANES] = value[g : g + 1, :]
    copy.wait()


def body(blocks, facets, observed, station_pairs, station_uvw, directions, fluxes, counts, jones_gains):
    f32 = jnp.float32
    stations = jones_gains.shape[3]
    cap = fluxes.shape[1]
    samples = observed.shape[2]
    share = observed.shape[3] // facets
    vmem = pl.BlockSpec(memory_space=VMEM)
    smem = pl.BlockSpec(memory_space=SMEM)
    facet = lax.axis_index("facet")
    width = -(-share // LANES) * LANES
    sliced = width == share
    if not sliced:
        pad = width - share
        observed = lax.dynamic_slice_in_dim(observed, facet * share, share, 3)
        station_pairs = lax.dynamic_slice_in_dim(station_pairs, facet * share, share, 1)
        observed = jnp.pad(observed, ((0, 0),) * 3 + ((0, pad),))
        station_pairs = jnp.pad(station_pairs, ((0, 0), (0, pad)), constant_values=-1)
    tile = (ROWS, stations // LANES, LANES)
    messages = message_counts(blocks, facets)
    dma = pltpu.SemaphoreType.DMA
    residual, totals = pl.pallas_call(
        functools.partial(calibrate_kernel, blocks, facets, sliced),
        out_shape=(jax.ShapeDtypeStruct((2, 4, samples, width), f32), jax.ShapeDtypeStruct(tile, f32)),
        in_specs=[pl.BlockSpec(memory_space=pl.ANY), vmem, vmem, vmem, vmem, smem, vmem],
        out_specs=(pl.BlockSpec(memory_space=pl.ANY), vmem),
        scratch_shapes=[
            pltpu.VMEM((2, 4, samples, width), f32),
            pltpu.VMEM((facets, 16, stations), f32),
            pltpu.VMEM((48, stations), f32),
            pltpu.VMEM((2, 32 + 8 * facets, width), f32),
            pltpu.VMEM((2, stations, width), jnp.bfloat16),
            pltpu.VMEM((8, TIMES * width), f32),
            pltpu.VMEM((4, cap, width), f32),
            pltpu.VMEM((facets, 2, samples, width), f32),
            pltpu.VMEM((2, 16 * facets, width), f32),
            pltpu.VMEM((facets,) + tile, f32),
            pltpu.VMEM((max(len(messages) - 1, 1),) + tile, f32),
        ]
        + [pltpu.VMEM((n,) + tile, f32) for n in messages]
        + [dma, dma, dma((facets - 1,)), dma((facets - 1,)), dma((sum(messages),)), dma((sum(messages),))],
        compiler_params=pltpu.CompilerParams(collective_id=0, has_side_effects=True),
        name="calibrate",
    )(observed, station_pairs, jnp.transpose(station_uvw, (1, 0, 2)), directions, fluxes, counts, jones_gains)
    anywhere = pl.BlockSpec(memory_space=pl.ANY)
    scaled, residual = pl.pallas_call(
        finish_kernel,
        out_shape=(jax.ShapeDtypeStruct((2, 4, 1, stations), f32), jax.ShapeDtypeStruct(residual.shape, f32)),
        in_specs=[vmem, anywhere],
        out_specs=(vmem, vmem),
        scratch_shapes=[dma],
        name="finish",
    )(totals, residual)
    if not sliced:
        residual = residual[..., :share]
    return residual, scaled


def solution(mesh):
    placed = (
        P(None, None, None, "base"),
        P(None, "base"),
        P(),
        P("facet", None, None),
        P("facet", None),
        P("facet"),
        P(None, None, "facet", None),
    )
    return jax.shard_map(
        functools.partial(body, mesh.shape["base"], mesh.shape["facet"]),
        mesh=mesh,
        in_specs=placed,
        out_specs=(P(None, None, None, ("base", "facet")), P(None, None, "facet", None)),
        check_vma=False,
    )
```
